256 devices in a mesh: ep: 64 (over z, x, core), etp: 4 (over y).
Axes of the slice: x: 4, y: 4, z: 8, core: 2. Of those that a mesh axis runs over, the one named last changes fastest.
Arguments:
- tokens: bfloat16 [8192, 6144], P('ep', 'etp'), may hold values from -6 to 6
- out_grad: bfloat16 [8192, 6144], P('ep', 'etp'), may hold values from -1.1953125 to 1.1953125
- probs: bfloat16 [8192, 2], P('ep'), may hold values from 0.049804688 to 0.94921875
- expert_ids: int32 [8192, 2], P('ep'), may hold values from 0 to 7, as said below
- slots: int32 [8192, 2], P('ep'), may hold values from -1 to 31, as said below
- counts: int32 [64, 8], P('ep'), may hold values from 0 to 128, as said below
- gate_weight: bfloat16 [6144, 16384], P('etp', 'ep'), may hold values from -0.078125 to 0.078125
- up_weight: bfloat16 [6144, 16384], P('etp', 'ep'), may hold values from -0.078125 to 0.078125
- down_weight: bfloat16 [16384, 6144], P('ep', 'etp'), may hold values from -0.0625 to 0.0625
Outputs:
- token_grad: bfloat16 [8192, 6144], P('ep', 'etp')
- prob_grad: float32 [8192, 2], P('ep')
- gate_grad: bfloat16 [6144, 16384], P('etp', 'ep')
- up_grad: bfloat16 [6144, 16384], P('etp', 'ep')
- down_grad: bfloat16 [16384, 6144], P('ep', 'etp')
The draws below stay inside these ranges and needn't reach their ends.
Inputs may be any that keep to these rules, and one draw needn't show every extreme that they name: `expert_ids`: each row names two different experts. `slots`: for assignment k of token t of index s of ep: the number of tokens of index s before t that name the same expert, or -1 when that number is 32 or more. counts[s,e] is the number of tokens of index s of ep that name expert e.
All inputs are finite; a program needn't handle non-finite values.
Results may differ from the reference program's by a relative error of at most 0.0058.
Values may be sent and summed in bfloat16 or wider, within the bound.
A program may use at most 128 MiB of HBM per device.

```python
import jax
import jax.numpy as jnp
from jax import lax

D = 6144
FFW = 8192
EXPERTS = 8
E_WIN = 2
TOK_DEV = 128
CAP = 32
TOKENS = 8192
N_EP = 64


def routing(key):
    key = jax.random.fold_in(key, 101)
    k_perm, k_one, k_two, k_off = jax.random.split(key, 4)
    ranking = jax.random.permutation(k_perm, EXPERTS)
    lowest = jnp.minimum(jax.random.randint(k_one, (TOKENS,), 0, EXPERTS), jax.random.randint(k_two, (TOKENS,), 0, EXPERTS))
    leader = ranking[lowest]
    position = jnp.arange(TOKENS, dtype=jnp.int32)
    leader = jnp.where(position < TOK_DEV, 0, leader)
    offset = jax.random.randint(k_off, (TOKENS,), 1, EXPERTS)
    second = (leader + offset) % EXPERTS
    return jnp.stack([leader, second], 1).astype(jnp.int32)


def tallies(key):
    chosen = routing(key)
    markers = (chosen[:, :, None] == jnp.arange(EXPERTS, dtype=jnp.int32)[None, None, :]).astype(jnp.int32)
    markers = markers.sum(1).reshape(TOKENS // TOK_DEV, TOK_DEV, EXPERTS)
    before = jnp.cumsum(markers, axis=1) - markers
    return (chosen, before.reshape(TOKENS, EXPERTS), markers.sum(1))


def draw_expert_ids(key, part):
    chosen, before, totals = tallies(key)
    return chosen


def draw_slots(key, part):
    chosen, before, totals = tallies(key)
    ranked = jnp.take_along_axis(before, chosen, axis=1)
    return jnp.where(ranked < CAP, ranked, -1).astype(jnp.int32)


def draw_counts(key, part):
    chosen, before, totals = tallies(key)
    return totals.astype(jnp.int32)


def levels(rng, dims, pieces, smallest, high):
    def one(dim, parts):
        steps = jax.random.uniform(jax.random.fold_in(jax.random.fold_in(rng, 6), dim), (parts,), jnp.float32, smallest / len(pieces), high / len(pieces))
        return jnp.repeat(jnp.exp(steps), dims[dim] // parts).reshape((-1,) + (1,) * (len(dims) - dim - 1))

    gain = one(*pieces[0])
    for cut in pieces[1:]:
        gain = gain * one(*cut)
    return gain


def gaussian(rng, shape, spread, most, pieces=(), kind=jnp.bfloat16):
    array = jax.random.normal(rng, shape, jnp.float32) * spread
    if len(pieces) > 0:
        array = levels(rng, shape, pieces, -0.22, 0.18) * array
    return jnp.clip(array, min=-most, max=most).astype(kind)


def setup_inputs(seed: int = 0) -> dict:
    arg_keys = jax.random.split(jax.random.key(seed), 10)
    return {
        "tokens": gaussian(arg_keys[0], (TOKENS, D), 1.0, 6.0, ((0, 64), (1, 4))),
        "out_grad": gaussian(arg_keys[1], (TOKENS, D), 0.2, 1.1953125, ((0, 64), (1, 4))),
        "probs": jnp.clip(0.049804688 + 0.89941406 * jax.random.uniform(arg_keys[2], (TOKENS, 2), jnp.float32) ** levels(arg_keys[2], (TOKENS, 2), ((0, 64),), -0.2, 0.2), 0.049804688, 0.94921875).astype(jnp.bfloat16),
        "expert_ids": draw_expert_ids(jax.random.fold_in(arg_keys[9], 71), 0),
        "slots": draw_slots(jax.random.fold_in(arg_keys[9], 71), 0),
        "counts": draw_counts(jax.random.fold_in(arg_keys[9], 71), 0),
        "gate_weight": gaussian(arg_keys[6], (D, E_WIN * FFW), D ** -0.5, 0.078125, ((0, 4), (1, 64))),
        "up_weight": gaussian(arg_keys[7], (D, E_WIN * FFW), D ** -0.5, 0.078125, ((0, 4), (1, 64))),
        "down_weight": gaussian(arg_keys[8], (E_WIN * FFW, D), FFW ** -0.5, 0.0625, ((0, 64), (1, 4))),
    }


def reference(tokens, out_grad, probs, expert_ids, slots, counts, gate_weight, up_weight, down_weight):
    groups = N_EP // E_WIN
    block = FFW // groups
    total = N_EP * CAP
    owner = jnp.arange(TOKENS, dtype=jnp.int32) // TOK_DEV
    limit = jnp.minimum(counts[owner[:, None], expert_ids], CAP)
    usable = (expert_ids < E_WIN) & (slots >= 0) & (slots < limit)
    target = owner[:, None] * CAP + slots
    source_rows = jnp.repeat(jnp.arange(TOKENS, dtype=jnp.int32), 2)
    token_acc = jnp.zeros((TOKENS, D), jnp.float32)
    prob_acc = jnp.zeros((TOKENS, 2), jnp.float32)
    gate_parts = []
    up_parts = []
    down_parts = []
    for expert in range(E_WIN):
        place = jnp.where(usable & (expert_ids == expert), target, total).astype(jnp.int32)
        flat_place = place.reshape(-1)
        x_slots = jnp.zeros((total, D), jnp.bfloat16).at[flat_place].set(tokens[source_rows], mode="drop")
        dy_slots = jnp.zeros((total, D), jnp.bfloat16).at[flat_place].set(out_grad[source_rows], mode="drop")
        p_slots = jnp.zeros((total,), jnp.bfloat16).at[flat_place].set(probs.reshape(-1), mode="drop")
        w_gate = gate_weight[:, expert * FFW:(expert + 1) * FFW]
        w_up = up_weight[:, expert * FFW:(expert + 1) * FFW]
        w_down = down_weight[expert * FFW:(expert + 1) * FFW, :]
        gate_vals = jnp.dot(x_slots, w_gate, preferred_element_type=jnp.float32)
        up_vals = jnp.dot(x_slots, w_up, preferred_element_type=jnp.float32)
        back_flow = jnp.dot(dy_slots, w_down.T, preferred_element_type=jnp.float32)
        sigma = jax.nn.sigmoid(gate_vals)
        activation = gate_vals * sigma * up_vals
        weight_p = p_slots.astype(jnp.float32)[:, None]
        weighted = (weight_p * activation).astype(jnp.bfloat16)
        gate_diff = (weight_p * back_flow * up_vals * sigma * (1.0 + gate_vals * (1.0 - sigma))).astype(jnp.bfloat16)
        up_diff = (weight_p * back_flow * gate_vals * sigma).astype(jnp.bfloat16)
        prob_blocks = jnp.sum((activation * back_flow).reshape(total, groups, block), axis=2).astype(jnp.bfloat16)
        prob_slot = jnp.sum(lax.optimization_barrier(prob_blocks).astype(jnp.float32), axis=1)

        def add_block(carry, index):
            begin = index * block
            gate_piece = lax.dynamic_slice_in_dim(gate_diff, begin, block, 1)
            up_piece = lax.dynamic_slice_in_dim(up_diff, begin, block, 1)
            gate_cols = lax.dynamic_slice_in_dim(w_gate, begin, block, 1)
            up_cols = lax.dynamic_slice_in_dim(w_up, begin, block, 1)
            part = jnp.dot(gate_piece, gate_cols.T, preferred_element_type=jnp.float32)
            part = part + jnp.dot(up_piece, up_cols.T, preferred_element_type=jnp.float32)
            part = lax.optimization_barrier(part.astype(jnp.bfloat16))
            return carry + part.astype(jnp.float32), None

        slot_sum, _ = lax.scan(add_block, jnp.zeros((total, D), jnp.float32), jnp.arange(groups, dtype=jnp.int32))
        gate_parts.append(jnp.dot(x_slots.T, gate_diff, preferred_element_type=jnp.float32).astype(jnp.bfloat16))
        up_parts.append(jnp.dot(x_slots.T, up_diff, preferred_element_type=jnp.float32).astype(jnp.bfloat16))
        down_parts.append(jnp.dot(weighted.T, dy_slots, preferred_element_type=jnp.float32).astype(jnp.bfloat16))
        padded = jnp.concatenate([slot_sum, jnp.zeros((1, D), jnp.float32)], 0)
        token_acc = token_acc + padded[place[:, 0]] + padded[place[:, 1]]
        prob_padded = jnp.concatenate([prob_slot, jnp.zeros((1,), jnp.float32)], 0)
        prob_acc = prob_acc + prob_padded[place]
    return (token_acc.astype(jnp.bfloat16), prob_acc, jnp.concatenate(gate_parts, 1),
            jnp.concatenate(up_parts, 1), jnp.concatenate(down_parts, 0))
```

```python
import jax
import jax.numpy as jnp
from jax import lax
from jax.experimental import pallas as pl
from jax.experimental.pallas import tpu as pltpu
from jax.sharding import PartitionSpec as P

E_WIN = 2
CAP = 32
BF = jnp.bfloat16
F32 = jnp.float32
NT = (((1,), (1,)), ((), ()))
TN = (((0,), (0,)), ((), ()))
ORDER = (
    (0, 1, 7, 2, 6, 3, 4, 5),
    (0, 1, 7, 2, 6, 3, 5, 4),
    (0, 7, 1, 6, 2, 5, 3, 4),
    (0, 7, 1, 6, 2, 5, 4, 3),
)
PROB = 128


def moe_kernel(
    xin, wg_hbm, wu_hbm, wd_hbm,
    out, gate_out, up_out, down_out,
    wg, wu, wd, xy, part, rss, rsr, diff, sp, r1r, sums, r2s, r2r, r3s, r3r, acc_pair, acc_down,
    w_sem, own_sem,
    zs_dn, zs_up, zs_other, z_recv, xs_up, xs_dn, x_recv, xf_send, x2_recv, sib_send, sib_recv,
    rs_send, rs_recv, ag_send, ag_recv, r1_send, r1_recv, r2_send, r2_recv, r3_send, r3_recv,
):
    feat = xin.shape[-1]
    hid = wg.shape[1]
    ep = lax.axis_index("ep")
    y = lax.axis_index("etp")
    core = lax.rem(ep, 2)
    x = lax.rem(ep // 2, 4)
    z = ep // 8
    zl = lax.rem(z, 4)
    group = z // 4

    def at(zz, xx, cc, yy):
        return ((zz * 4 + xx) * 2 + cc, yy)

    def z_dev(shift):
        return at(lax.rem(z + shift, 8), x, core, y)

    x_up = at(z, lax.rem(x + 1, 4), core, y)
    x_dn = at(z, lax.rem(x + 3, 4), core, y)
    sibling = at(z, x, 1 - core, y)
    q_up = lax.rem(y + 1, 4)
    q_dn = lax.rem(y + 3, 4)
    q_op = lax.rem(y + 2, 4)
    y_up = (ep, q_up)
    y_dn = (ep, q_dn)

    sends = []

    def remote(src, dst, send_sem, recv_sem, dev):
        return pltpu.make_async_remote_copy(
            src_ref=src, dst_ref=dst, send_sem=send_sem, recv_sem=recv_sem,
            device_id=dev, device_id_type=pl.DeviceIdType.MESH,
        )

    def push(src, dst, send_sem, recv_sem, dev):
        copy = remote(src, dst, send_sem, recv_sem, dev)
        copy.start()
        sends.append((None, copy))

    def arrive(dst, recv_sem):
        remote(dst, dst, own_sem, recv_sem, sibling).wait_recv()

    barrier = pltpu.get_barrier_semaphore()
    partners = [z_dev(s) for s in range(1, 8)] + [x_up, x_dn, y_up, y_dn, sibling]
    for dev in partners:
        pl.semaphore_signal(barrier, inc=1, device_id=dev, device_id_type=pl.DeviceIdType.MESH)
    w_copies = [
        pltpu.make_async_copy(src, dst, w_sem.at[i])
        for i, (src, dst) in enumerate(((wg_hbm, wg), (wu_hbm, wu), (wd_hbm, wd)))
    ]
    for copy in w_copies:
        copy.start()
    xy[:, 0, 0, 0] = xin[group]
    pl.semaphore_wait(barrier, len(partners))

    def z_branch(v, k):
        r = ORDER[v][k]
        src = xy.at[:, k, 0, 0]
        down = r <= 5 - v
        todo = []
        if (down or r == 0) and v > 0:
            to = ORDER[v - 1].index(r + 1)
            todo.append(
                lambda: remote(src, xy.at[:, to, 0, 0], zs_dn.at[k], z_recv.at[to], z_dev(7))
            )
        if (not down or r == 0) and v < 3:
            back_to = ORDER[v + 1].index((r + 7) % 8)
            todo.append(
                lambda: remote(src, xy.at[:, back_to, 0, 0], zs_up.at[k], z_recv.at[back_to], z_dev(1))
            )
        if k == 0:
            if v <= 1:
                w, far, shift = 3, v + 1, 7 - v
            else:
                w, far, shift = 0, 8 - (4 - v), 4 - v
            slot = ORDER[w].index(far)
            todo.append(
                lambda: remote(
                    xin.at[1 - group], xy.at[:, slot, 0, 0], zs_other, z_recv.at[slot], z_dev(shift)
                )
            )
        return todo

    def z_step(k):
        if k > 0:
            arrive(xy.at[:, k, 0, 0], z_recv.at[k])
        for v in range(4):
            todo = z_branch(v, k)
            if todo:
                def run(todo=todo):
                    for make in todo:
                        make().start()

                pl.when(zl == v)(run)
                sends.append((v, todo))
        src = xy.at[:, k, 0, 0]
        push(src, xy.at[:, k, 0, 1], xs_up.at[k], x_recv.at[0, k], x_up)
        push(src, xy.at[:, k, 0, 2], xs_dn.at[k], x_recv.at[1, k], x_dn)

    def x_step(k):
        arrive(xy.at[:, k, 0, 1], x_recv.at[0, k])
        if k % 2 == 0:
            push(xy.at[:, k, 0, 1], xy.at[:, k, 0, 3], xf_send.at[k], x2_recv.at[k], x_up)
        arrive(xy.at[:, k, 0, 2], x_recv.at[1, k])
        if k % 2 == 1:
            push(xy.at[:, k, 0, 2], xy.at[:, k, 0, 3], xf_send.at[k], x2_recv.at[k], x_dn)

    def sib_step(k):
        arrive(xy.at[:, k, 0, 3], x2_recv.at[k])
        push(xy.at[:, k, 0], xy.at[:, k, 1], sib_send.at[k], sib_recv.at[k], sibling)

    def sib_wait(k):
        arrive(xy.at[:, k, 1], sib_recv.at[k])

    def partial_sums(j):
        if j == 0:
            for copy in w_copies:
                copy.wait()

        def body(p, carry):
            xs = xy[0, 2 * j + p].reshape(8 * CAP, feat)
            dys = xy[1, 2 * j + p].reshape(8 * CAP, feat)
            rows = pl.ds(2 * p, 2)
            b = j % 2
            part[b, rows, :, 0:hid] = jnp.dot(
                xs, wg[...], preferred_element_type=F32).reshape(2, 4 * CAP, hid)
            part[b, rows, :, hid:2 * hid] = jnp.dot(
                xs, wu[...], preferred_element_type=F32).reshape(2, 4 * CAP, hid)
            part[b, rows, :, 2 * hid:3 * hid] = lax.dot_general(
                dys, wd[...], NT, preferred_element_type=F32).reshape(2, 4 * CAP, hid)
            return carry

        lax.fori_loop(0, 2, body, 0)

    LO, HI = slice(0, 64), slice(64, 128)

    def rs_a(j):
        b = j % 2
        for slot, (q, half, dev) in enumerate(
            ((q_op, LO, y_up), (q_op, HI, y_dn), (q_up, HI, y_up), (q_dn, LO, y_dn))
        ):
            rss[j, slot] = part[b, q, half].astype(BF)
            push(rss.at[j, slot], rsr.at[j, slot], rs_send.at[j, slot], rs_recv.at[j, slot], dev)

    def rs_b(j):
        b = j % 2
        for slot, (q, half, dev) in ((4, (q_up, LO, y_up)), (5, (q_dn, HI, y_dn))):
            arrive(rsr.at[j, slot - 4], rs_recv.at[j, slot - 4])
            rss[j, slot] = (part[b, q, half] + rsr[j, slot - 4].astype(F32)).astype(BF)
            push(rss.at[j, slot], rsr.at[j, slot], rs_send.at[j, slot], rs_recv.at[j, slot], dev)

    def rs_c(j):
        b = j % 2
        for slot in range(2, 6):
            arrive(rsr.at[j, slot], rs_recv.at[j, slot])
        for half, one, two in ((LO, 4, 3), (HI, 2, 5)):
            total = part[b, y, half] + rsr[j, one].astype(F32) + rsr[j, two].astype(F32)
            gate = total[:, 0:hid]
            up = total[:, hid:2 * hid]
            back = total[:, 2 * hid:3 * hid]
            sg = jax.nn.sigmoid(gate)
            silu = gate * sg
            act = silu * up
            diff[j, y, half, 0:hid] = (back * up * sg * (1.0 + gate * (1.0 - sg))).astype(BF)
            diff[j, y, half, hid:2 * hid] = (back * silu).astype(BF)
            diff[j, y, half, 2 * hid:3 * hid] = act.astype(BF)
            prob = act * back
            lanes = prob[:, 0:PROB]
            for i in range(1, hid // PROB):
                lanes = lanes + prob[:, i * PROB:(i + 1) * PROB]
            diff[j, y, half, 3 * hid:] = lanes.astype(BF)
        for i, half in enumerate((LO, HI)):
            src = diff.at[j, y, half]
            push(src, src, ag_send.at[j, i], ag_recv.at[j, i], y_up)
            push(src, src, ag_send.at[j, 2 + i], ag_recv.at[j, 2 + i], y_dn)

    def ag_b(j):
        lo = diff.at[j, q_dn, LO]
        arrive(lo, ag_recv.at[j, 0])
        push(lo, lo, ag_send.at[j, 4], ag_recv.at[j, 4], y_up)
        hi = diff.at[j, q_up, HI]
        arrive(hi, ag_recv.at[j, 3])
        push(hi, hi, ag_send.at[j, 5], ag_recv.at[j, 5], y_dn)

    def ag_c(j):
        arrive(diff.at[j, q_dn, HI], ag_recv.at[j, 1])
        arrive(diff.at[j, q_up, LO], ag_recv.at[j, 2])
        arrive(diff.at[j, q_op, LO], ag_recv.at[j, 4])
        arrive(diff.at[j, q_op, HI], ag_recv.at[j, 5])

    def slot_rows(j):
        def rows_of(p, side):
            d = diff[j, 2 * p + side]
            value = lax.dot_general(d[:, 0:hid], wg[...], NT, preferred_element_type=F32)
            value = value + lax.dot_general(
                d[:, hid:2 * hid], wu[...], NT, preferred_element_type=F32)
            return value, d[:, 3 * hid:]

        def theirs(p, carry):
            value, prob = rows_of(p, 1)
            sp[j, p, :, 0:feat] = value.astype(BF)
            sp[j, p, :, feat:] = prob
            return carry

        def mine(p, carry):
            value, prob = rows_of(p, 0)
            sums[j % 2, p, :, 0:feat] = value
            sums[j % 2, p, :, feat:] = prob.astype(F32)
            return carry

        lax.fori_loop(0, 2, theirs, 0)
        push(sp.at[j], r1r.at[j], r1_send.at[j], r1_recv.at[j], sibling)
        lax.fori_loop(0, 2, mine, 0)

    def rel(i):
        return slice(i * CAP, (i + 1) * CAP)

    def r2_a(j):
        b = j % 2
        arrive(r1r.at[j], r1_recv.at[j])
        sums[b] = sums[b] + r1r[j].astype(F32)
        for slot, (p, i, dev) in enumerate(
            ((0, 3, x_up), (1, 3, x_dn), (1, 2, x_up), (0, 1, x_dn))
        ):
            r2s[j, slot] = sums[b, p, rel(i)].astype(BF)
            push(r2s.at[j, slot], r2r.at[j, slot], r2_send.at[j, slot], r2_recv.at[j, slot], dev)

    def r2_b(j):
        b = j % 2
        for slot, (p, i, dev) in ((4, (0, 2, x_up)), (5, (1, 1, x_dn))):
            arrive(r2r.at[j, slot - 4], r2_recv.at[j, slot - 4])
            r2s[j, slot] = (sums[b, p, rel(i)] + r2r[j, slot - 4].astype(F32)).astype(BF)
            push(r2s.at[j, slot], r2r.at[j, slot], r2_send.at[j, slot], r2_recv.at[j, slot], dev)

    def r2_c(j):
        b = j % 2
        for slot in range(2, 6):
            arrive(r2r.at[j, slot], r2_recv.at[j, slot])
        for p, one, two in ((0, 4, 3), (1, 2, 5)):
            k = 2 * j + p
            total = sums[b, p, rel(0)] + r2r[j, one].astype(F32) + r2r[j, two].astype(F32)
            if k == 0:
                r3r[0] = total.astype(BF)
                continue
            r3s[k] = total.astype(BF)
            for v in range(4):
                r = ORDER[v][k]
                s = 8 - r
                todo = [lambda r=r, s=s, k=k: remote(
                    r3s.at[k], r3r.at[s], r3_send.at[k], r3_recv.at[s], z_dev(r))]

                def run(todo=todo):
                    for make in todo:
                        make().start()

                pl.when(zl == v)(run)
                sends.append((v, todo))

    tile = 256

    def grads(j):
        def pair_body(t, carry):
            cols = pl.ds(pl.multiple_of(t * tile, tile), tile)
            xs = xy[0, 2 * j:2 * j + 2, :, :, :, cols].reshape(16 * CAP, tile)
            d = diff[j, :, :, 0:2 * hid].reshape(16 * CAP, 2 * hid)
            new = lax.dot_general(xs, d, TN, preferred_element_type=F32)
            if j == 0:
                acc_pair[cols, :] = new
            elif j < 3:
                acc_pair[cols, :] += new
            else:
                new = new + acc_pair[cols, :]
                gate_out[cols, :] = new[:, 0:hid].astype(BF)
                up_out[cols, :] = new[:, hid:].astype(BF)
            return carry

        def down_body(t, carry):
            cols = pl.ds(pl.multiple_of(t * tile, tile), tile)
            dys = xy[1, 2 * j:2 * j + 2, :, :, :, cols].reshape(16 * CAP, tile)
            act = diff[j, :, :, 2 * hid:3 * hid].reshape(16 * CAP, hid)
            new = lax.dot_general(act, dys, TN, preferred_element_type=F32)
            if j == 0:
                acc_down[:, cols] = new
            elif j < 3:
                acc_down[:, cols] += new
            else:
                down_out[:, cols] = (new + acc_down[:, cols]).astype(BF)
            return carry

        lax.fori_loop(0, feat // tile, pair_body, 0)
        lax.fori_loop(0, feat // tile, down_body, 0)

    for tick in range(19):
        if tick < 8:
            z_step(tick)
        if 0 <= tick - 1 < 8:
            x_step(tick - 1)
        if 0 <= tick - 2 < 8:
            sib_step(tick - 2)
        for lag, stage in (
            (5, rs_b), (6, rs_c), (7, ag_b), (9, r2_a), (10, r2_b), (11, r2_c)
        ):
            j, odd = divmod(tick - lag, 2)
            if odd == 0 and 0 <= j < 4:
                stage(j)
        if 0 <= tick - 3 < 8:
            sib_wait(tick - 3)
        j, odd = divmod(tick - 4, 2)
        if odd == 0 and 0 <= j < 4:
            partial_sums(j)
            rs_a(j)
        j, odd = divmod(tick - 8, 2)
        if odd == 0 and 0 <= j < 4:
            ag_c(j)
            slot_rows(j)
        j, odd = divmod(tick - 9, 2)
        if odd == 0 and 0 <= j < 4:
            grads(j)

    out[...] = jnp.zeros_like(out)
    for s in range(8):
        if s > 0:
            arrive(r3r.at[s], r3_recv.at[s])
        owner = lax.rem(z + s, 8) // 4
        out[owner] = out[owner] + r3r[s].astype(F32)
    for v, item in sends:
        if v is None:
            item.wait_send()
        else:
            def run(item=item):
                for make in item:
                    make().wait_send()

            pl.when(zl == v)(run)


def moe(xin, gate_weight, up_weight, down_weight):
    feat, hid = gate_weight.shape
    width = 3 * hid + PROB
    wide = feat + PROB
    dma = pltpu.SemaphoreType.DMA
    vmem = pl.BlockSpec(memory_space=pltpu.VMEM)
    hbm = pl.BlockSpec(memory_space=pl.ANY)
    return pl.pallas_call(
        moe_kernel,
        out_shape=(
            jax.ShapeDtypeStruct((E_WIN, CAP, wide), F32),
            jax.ShapeDtypeStruct((feat, hid), BF),
            jax.ShapeDtypeStruct((feat, hid), BF),
            jax.ShapeDtypeStruct((hid, feat), BF),
        ),
        in_specs=[vmem, hbm, hbm, hbm],
        out_specs=(vmem, vmem, vmem, vmem),
        scratch_shapes=[
            pltpu.VMEM((feat, hid), BF),
            pltpu.VMEM((feat, hid), BF),
            pltpu.VMEM((hid, feat), BF),
            pltpu.VMEM((2, 8, 2, 4, CAP, feat), BF),
            pltpu.VMEM((2, 4, 4 * CAP, 3 * hid), F32),
            pltpu.VMEM((4, 6, 2 * CAP, 3 * hid), BF),
            pltpu.VMEM((4, 6, 2 * CAP, 3 * hid), BF),
            pltpu.VMEM((4, 4, 4 * CAP, width), BF),
            pltpu.VMEM((4, 2, 4 * CAP, wide), BF),
            pltpu.VMEM((4, 2, 4 * CAP, wide), BF),
            pltpu.VMEM((2, 2, 4 * CAP, wide), F32),
            pltpu.VMEM((4, 6, CAP, wide), BF),
            pltpu.VMEM((4, 6, CAP, wide), BF),
            pltpu.VMEM((8, CAP, wide), BF),
            pltpu.VMEM((8, CAP, wide), BF),
            pltpu.VMEM((feat, 2 * hid), F32),
            pltpu.VMEM((hid, feat), F32),
            dma((3,)), dma,
            dma((8,)), dma((8,)), dma, dma((8,)),
            dma((8,)), dma((8,)), dma((2, 8)), dma((8,)), dma((8,)), dma((8,)), dma((8,)),
            dma((4, 6)), dma((4, 6)), dma((4, 6)), dma((4, 6)),
            dma((4,)), dma((4,)), dma((4, 6)), dma((4, 6)), dma((8,)), dma((8,)),
        ],
        compiler_params=pltpu.CompilerParams(
            collective_id=0, has_side_effects=True, vmem_limit_bytes=62 * 1024 * 1024
        ),
        cost_estimate=pl.CostEstimate(
            flops=13 * 10**9, bytes_accessed=8 * 10**6, transcendentals=0
        ),
    )(xin, gate_weight, up_weight, down_weight)


def shards(tokens, out_grad, probs, expert_ids, slots, counts, gate_weight, up_weight, down_weight):
    feature_cols = tokens.shape[1]
    slot_rows = E_WIN * CAP
    expert_table = jnp.arange(counts.shape[1], dtype=jnp.int32)
    limit = jnp.sum(
        jnp.where(
            expert_ids[:, :, None] == expert_table[None, None, :], counts[0][None, None, :], 0
        ),
        axis=2,
    )
    usable = (expert_ids < E_WIN) & (slots >= 0) & (slots < jnp.minimum(limit, CAP))
    target = jnp.where(usable, expert_ids * CAP + slots, -1)
    pick_map = jnp.arange(slot_rows, dtype=jnp.int32)[:, None, None] == target[None, :, :]
    selector = jnp.sum(pick_map.astype(F32), axis=2)
    scaled = jnp.sum(jnp.where(pick_map, probs.astype(F32)[None], 0.0), axis=2)
    x_rows = jnp.dot(selector.astype(BF), tokens, preferred_element_type=F32).astype(BF)
    dy_rows = jnp.dot(scaled.astype(BF), out_grad, preferred_element_type=F32).astype(BF)
    xin = jnp.stack(
        [x_rows.reshape(E_WIN, CAP, feature_cols), dy_rows.reshape(E_WIN, CAP, feature_cols)], 1
    )
    rows, gate_grad, up_grad, down_grad = moe(xin, gate_weight, up_weight, down_weight)
    rows = rows.reshape(slot_rows, feature_cols + PROB)
    token_grad = lax.dot_general(
        selector,
        rows[:, :feature_cols],
        TN,
        precision=lax.Precision.HIGHEST,
        preferred_element_type=F32,
    ).astype(BF)
    summed_p = jnp.sum(rows[:, feature_cols:], axis=1)
    picked = jnp.sum(jnp.where(pick_map, summed_p[:, None, None], 0.0), axis=0)
    prob_grad = picked / probs.astype(F32)
    return (token_grad, prob_grad, gate_grad, up_grad, down_grad)


def solution(mesh):
    in_specs = (
        P("ep", "etp"),
        P("ep", "etp"),
        P("ep", None),
        P("ep", None),
        P("ep", None),
        P("ep", None),
        P("etp", "ep"),
        P("etp", "ep"),
        P("ep", "etp"),
    )
    out_specs = (P("ep", "etp"), P("ep", None), P("etp", "ep"), P("etp", "ep"), P("ep", "etp"))
    return jax.shard_map(shards, mesh=mesh, in_specs=in_specs, out_specs=out_specs, check_vma=False)
```
